32 devices in a mesh: dp: 4 (over z), tensor: 8 (over y, x, core).
Axes of the slice: x: 2, y: 2, z: 4, core: 2. Of those that a mesh axis runs over, the one named last changes fastest.
Arguments:
- tokens: bfloat16 [512, 8192], P('dp'), may hold values from -6 to 6
- hidden_grad: bfloat16 [512, 14336], P('dp', 'tensor'), may hold values from -6 to 6
- gate_weight: bfloat16 [8192, 14336], P('dp', 'tensor'), may hold values from -0.0625 to 0.0625
- up_weight: bfloat16 [8192, 14336], P('dp', 'tensor'), may hold values from -0.0625 to 0.0625
- proj_in: bfloat16 [2, 8192, 64], P(None, 'tensor'), may hold values from -0.005859375 to 0.005859375
- proj_out: bfloat16 [2, 14336, 64], P(None, 'tensor'), may hold values from -0.046875 to 0.046875
Outputs:
- input_grad: bfloat16 [512, 8192], P('dp', 'tensor')
- features: float32 [4, 2, 64, 64], P('dp', None, 'tensor')
The draws below stay inside these ranges and needn't reach their ends.
All inputs are finite; a program needn't handle non-finite values.
Results may differ from the reference program's by a relative error of at most 0.012.
Values may be sent and summed in bfloat16 or wider, within the bound.
A program may use at most 192 MiB of HBM per device.

```python
import jax
import jax.numpy as jnp
from jax import lax

D = 8192
FF = 14336
RANK = 64
SEQ_LEN = 128
SEQS = 4
TOKENS = 512
N_TENSOR = 8


def level_of(own_key, dims, split, low, top_value):
    level = 1.0
    for axis_at, shards_of in split:
        steps = jax.random.uniform(jax.random.fold_in(jax.random.fold_in(own_key, 6), axis_at), (shards_of,), jnp.float32, low / len(split), top_value / len(split))
        level = level * jnp.repeat(jnp.exp(steps), dims[axis_at] // shards_of).reshape((-1,) + (1,) * (len(dims) - 1 - axis_at))
    return level


def noise(stream_key, extent, spread, limit, pieces=(), kind=jnp.bfloat16):
    result = jax.random.normal(stream_key, extent, jnp.float32) * spread
    if len(pieces) > 0:
        result = level_of(stream_key, extent, pieces, -0.22, 0.18) * result
    return jnp.clip(result, min=-limit, max=limit).astype(kind)


def setup_inputs(seed: int = 0) -> dict:
    key_of = jax.random.split(jax.random.key(seed), 7)
    tokens = noise(key_of[0], (TOKENS, D), 1.0, 6.0, ((0, 4),))
    hidden_grad = noise(key_of[1], (TOKENS, FF), 1.0, 6.0, ((0, 4), (1, 8)))
    gate_weight = noise(key_of[2], (D, FF), D ** -0.5, 0.0625, ((0, 4), (1, 8)))
    up_weight = noise(key_of[3], (D, FF), D ** -0.5, 0.0625, ((0, 4), (1, 8)))
    proj_in = noise(key_of[4], (2, D, RANK), (D * SEQ_LEN) ** -0.5, 0.005859375, ((1, 8),))
    proj_out = noise(key_of[5], (2, FF, RANK), FF ** -0.5, 0.046875, ((1, 8),))
    return {"tokens": tokens, "hidden_grad": hidden_grad, "gate_weight": gate_weight, "up_weight": up_weight, "proj_in": proj_in, "proj_out": proj_out}


def reference(tokens, hidden_grad, gate_weight, up_weight, proj_in, proj_out):
    width = FF // N_TENSOR
    highest = lax.Precision.HIGHEST

    def slab(carry, group):
        total, grad_sum = carry
        start = group * width
        w_gate = lax.dynamic_slice_in_dim(gate_weight, start, width, 1)
        w_up = lax.dynamic_slice_in_dim(up_weight, start, width, 1)
        cotan = lax.dynamic_slice_in_dim(hidden_grad, start, width, 1).astype(jnp.float32)
        out_proj = lax.dynamic_slice_in_dim(proj_out, start, width, 1).astype(jnp.float32)
        gate = jnp.dot(tokens, w_gate, preferred_element_type=jnp.float32)
        up = jnp.dot(tokens, w_up, preferred_element_type=jnp.float32)
        sigm = jax.nn.sigmoid(gate)
        d_gate = (cotan * up * sigm * (1.0 + gate * (1.0 - sigm))).astype(jnp.bfloat16)
        d_up = (cotan * gate * sigm).astype(jnp.bfloat16)
        part = jnp.dot(d_gate, w_gate.T, preferred_element_type=jnp.float32)
        part = part + jnp.dot(d_up, w_up.T, preferred_element_type=jnp.float32)
        part = lax.optimization_barrier(part.astype(jnp.bfloat16)).astype(jnp.float32)
        grads = jnp.stack([
            jnp.dot(d_gate.astype(jnp.float32), out_proj[0], precision=highest),
            jnp.dot(d_up.astype(jnp.float32), out_proj[1], precision=highest)], axis=1)
        return (total + part, grad_sum + grads), None

    start_carry = (jnp.zeros((TOKENS, D), jnp.float32), jnp.zeros((TOKENS, 2, RANK), jnp.float32))
    (total, grad_sum), unused = lax.scan(slab, start_carry, jnp.arange(N_TENSOR, dtype=jnp.int32))
    input_grad = total.astype(jnp.bfloat16)
    projected_in = jnp.einsum("td,kda->tka", tokens.astype(jnp.float32), proj_in.astype(jnp.float32), precision=highest)
    seq_in = projected_in.reshape(SEQS, SEQ_LEN, 2, RANK)
    seq_grad = grad_sum.reshape(SEQS, SEQ_LEN, 2, RANK)
    features = jnp.einsum("slka,slkb->skab", seq_in, seq_grad, precision=highest)
    return input_grad, features
```

```python
import jax
import jax.numpy as jnp
from jax import lax
from jax.sharding import PartitionSpec as P

SEQ_LEN = 128
F32 = jnp.float32
BF16 = jnp.bfloat16


def shards(n_dp, n_tensor, tokens, hidden_grad, gate_weight, up_weight, proj_in, proj_out):
    highest = lax.Precision.HIGHEST
    place = lax.axis_index("tensor")
    rows, width = tokens.shape
    rank = proj_in.shape[2]
    block = width // n_dp
    band = width // n_tensor
    halves = n_tensor // n_dp
    share = rows // n_tensor

    mine = lax.dynamic_slice_in_dim(tokens, place * share, share, 0)
    mine = mine.reshape(share, n_dp, block).transpose(1, 0, 2)
    mine = lax.all_to_all(mine, "dp", 0, 0)
    tok = lax.all_gather(mine, "tensor", axis=1, tiled=True).reshape(n_dp * rows, block)

    gate_part = jnp.dot(tok, gate_weight, preferred_element_type=F32).astype(BF16)
    up_part = jnp.dot(tok, up_weight, preferred_element_type=F32).astype(BF16)
    gate = lax.psum_scatter(gate_part, "dp", scatter_dimension=0, tiled=True).astype(F32)
    up = lax.psum_scatter(up_part, "dp", scatter_dimension=0, tiled=True).astype(F32)
    cotan = hidden_grad.astype(F32)
    sigm = jax.nn.sigmoid(gate)
    d_gate = (cotan * up * sigm * (1.0 + gate * (1.0 - sigm))).astype(BF16)
    d_up = (cotan * gate * sigm).astype(BF16)
    d_gate_all = lax.all_gather(d_gate, "dp", axis=0, tiled=True)
    d_up_all = lax.all_gather(d_up, "dp", axis=0, tiled=True)
    term = jnp.einsum("tf,df->td", d_gate_all, gate_weight, preferred_element_type=F32)
    term = (term + jnp.einsum("tf,df->td", d_up_all, up_weight, preferred_element_type=F32)).astype(BF16)
    term = term.reshape(n_dp, rows, halves, band).transpose(0, 2, 1, 3).reshape(n_tensor * rows, band)
    piece = lax.psum_scatter(term, "tensor", scatter_dimension=0, tiled=True)
    pairs = []
    for i in range(n_dp):
        for m in range(n_tensor):
            p, h = divmod(m, halves)
            pairs.append((i * n_tensor + m, p * n_tensor + i * halves + h))
    input_grad = lax.ppermute(piece, ("dp", "tensor"), pairs)

    local_cols = lax.dynamic_slice_in_dim(tokens, place * band, band, 1)
    in_partial = jnp.einsum("td,kda->tka", local_cols, proj_in, preferred_element_type=F32)
    projected_in = lax.psum(in_partial, "tensor")
    grad_partial = jnp.stack(
        [
            jnp.dot(d_gate, proj_out[0], preferred_element_type=F32),
            jnp.dot(d_up, proj_out[1], preferred_element_type=F32),
        ],
        axis=1,
    )
    seqs = rows // SEQ_LEN
    seq_in = projected_in.reshape(seqs, SEQ_LEN, 2, rank)
    seq_grad = grad_partial.reshape(seqs, SEQ_LEN, 2, rank)
    terms = jnp.einsum("slka,slkb->skab", seq_in, seq_grad, precision=highest)
    features = lax.psum_scatter(terms, "tensor", scatter_dimension=2, tiled=True)
    return (input_grad, features)


def solution(mesh):
    placed = (
        P("dp", None),
        P("dp", "tensor"),
        P("dp", "tensor"),
        P("dp", "tensor"),
        P(None, "tensor", None),
        P(None, "tensor", None),
    )

    def body(*args):
        return shards(mesh.shape["dp"], mesh.shape["tensor"], *args)

    return jax.shard_map(
        body,
        mesh=mesh,
        in_specs=placed,
        out_specs=(P("dp", "tensor"), P("dp", None, "tensor", None)),
        check_vma=False,
    )
```

```python
import functools

import jax
import jax.numpy as jnp
from jax import lax
from jax.experimental import pallas as pl
from jax.experimental.pallas import tpu as pltpu
from jax.sharding import PartitionSpec as P

SEQ_LEN = 128
F32 = jnp.float32
BF16 = jnp.bfloat16


def shards(n_dp, n_tensor, tokens, hidden_grad, gate_weight, up_weight, proj_in, proj_out):
    highest = lax.Precision.HIGHEST
    place = lax.axis_index("tensor")
    rows, width = tokens.shape
    rank = proj_in.shape[2]
    block = width // n_dp
    band = width // n_tensor
    halves = n_tensor // n_dp
    share = rows // n_tensor

    mine = lax.dynamic_slice_in_dim(tokens, place * share, share, 0)
    mine = mine.reshape(share, n_dp, block).transpose(1, 0, 2)
    mine = lax.all_to_all(mine, "dp", 0, 0)
    tok = lax.all_gather(mine, "tensor", axis=1, tiled=True).reshape(n_dp * rows, block)

    gate_part = jnp.dot(tok, gate_weight, preferred_element_type=F32).astype(BF16)
    up_part = jnp.dot(tok, up_weight, preferred_element_type=F32).astype(BF16)
    gate = lax.psum_scatter(gate_part, "dp", scatter_dimension=0, tiled=True).astype(F32)
    up = lax.psum_scatter(up_part, "dp", scatter_dimension=0, tiled=True).astype(F32)
    cotan = hidden_grad.astype(F32)
    sigm = jax.nn.sigmoid(gate)
    d_gate = (cotan * up * sigm * (1.0 + gate * (1.0 - sigm))).astype(BF16)
    d_up = (cotan * gate * sigm).astype(BF16)
    d_gate_all = lax.all_gather(d_gate, "dp", axis=0, tiled=True)
    d_up_all = lax.all_gather(d_up, "dp", axis=0, tiled=True)
    term = jnp.einsum("tf,df->td", d_gate_all, gate_weight, preferred_element_type=F32)
    term = (term + jnp.einsum("tf,df->td", d_up_all, up_weight, preferred_element_type=F32)).astype(BF16)
    term = term.reshape(n_dp, rows, halves, band).transpose(0, 2, 1, 3).reshape(n_tensor * rows, band)
    piece = lax.psum_scatter(term, "tensor", scatter_dimension=0, tiled=True)
    pairs = []
    for i in range(n_dp):
        for m in range(n_tensor):
            p, h = divmod(m, halves)
            pairs.append((i * n_tensor + m, p * n_tensor + i * halves + h))
    input_grad = lax.ppermute(piece, ("dp", "tensor"), pairs)

    local_cols = lax.dynamic_slice_in_dim(tokens, place * band, band, 1)
    in_partial = jnp.einsum("td,kda->tka", local_cols, proj_in, preferred_element_type=F32)
    projected_in = lax.psum(in_partial, "tensor")
    grad_partial = jnp.stack(
        [
            jnp.dot(d_gate, proj_out[0], preferred_element_type=F32),
            jnp.dot(d_up, proj_out[1], preferred_element_type=F32),
        ],
        axis=1,
    )
    seqs = rows // SEQ_LEN
    seq_in = projected_in.reshape(seqs, SEQ_LEN, 2, rank)
    seq_grad = grad_partial.reshape(seqs, SEQ_LEN, 2, rank)
    terms = jnp.einsum("slka,slkb->skab", seq_in, seq_grad, precision=highest)
    features = lax.psum_scatter(terms, "tensor", scatter_dimension=2, tiled=True)
    return (input_grad, features)


ROUND = 16
TILE = 256
NDP = 4
NT = 8


def fused(
    tokens, hidden, gate_hbm, up_hbm, proj_in, proj_out, grad_out, feat_out,
    wg, wu, tok, acc, part, recv, dval, term, landed, fin, fin_land,
    pin_send, pin_recv, pin_all, feat_send, feat_recv,
    w_sem, a1_send, a1_recv, a2_send, a2_recv, red_send, red_recv,
    root_send, fwd_send, bc_recv, rs_send, rs_recv, fin_send, fin_recv,
    ps_send, ps_recv, pa_send, pa_recv, ft_send, ft_recv,
):
    z, t = lax.axis_index("dp"), lax.axis_index("tensor")
    rows, width = tokens.shape
    block, hid = wg.shape
    band = width // NT
    rank = proj_in.shape[2]
    share = rows // NT
    rounds = rows // ROUND
    brows = 2 * ROUND
    mid = jnp.logical_and(z > 0, z < NDP - 1)
    edge = jnp.logical_or(z == 0, z == NDP - 1)
    low = z // 2
    o0 = 3 - 3 * low
    o2 = z + 1 - 2 * low
    o1 = 6 - z - o0 - o2
    ways = (1 - 2 * low, 1 - 2 * (z % 2), 1 - 2 * low)
    dests = (o0, o1, o2)
    is1 = (z % 2) * (1 - low)
    slots = (o0, o1 + (4 - o1) * is1, o2 + (4 - o2) * low)
    pz, pt = t // 2, 2 * z + t % 2
    away = pz != z

    def remote(src, dst, ssem, rsem, dz, dt):
        return pltpu.make_async_remote_copy(
            src_ref=src, dst_ref=dst, send_sem=ssem, recv_sem=rsem,
            device_id=(dz, dt), device_id_type=pl.DeviceIdType.MESH,
        )

    def drain(ref, sem):
        pltpu.make_async_copy(ref, ref, sem).wait()

    def peers(fn):
        def step(d, c):
            fn(lax.rem(t + d, NT))
            return c

        lax.fori_loop(1, NT, step, 0)

    cg = pltpu.make_async_copy(gate_hbm, wg, w_sem.at[0])
    cu = pltpu.make_async_copy(up_hbm, wu, w_sem.at[1])
    cg.start()
    cu.start()

    barrier = pltpu.get_barrier_semaphore()

    def hello(dz, dt):
        pl.semaphore_signal(barrier, inc=1, device_id=(dz, dt), device_id_type=pl.DeviceIdType.MESH)

    peers(lambda q: hello(z, q))
    for d in range(1, NDP):
        hello(lax.rem(z + d, NDP), t)

    @pl.when(away)
    def _():
        hello(pz, pt)
        pl.semaphore_wait(barrier, NT + NDP - 1)

    @pl.when(jnp.logical_not(away))
    def _():
        pl.semaphore_wait(barrier, NT + NDP - 2)

    my_rows = pl.ds(pl.multiple_of(t * share, share), share)
    for d in range(1, NDP):
        i = lax.rem(z + d, NDP)
        remote(
            tokens.at[my_rows, pl.ds(pl.multiple_of(i * block, block), block)],
            tok.at[z, my_rows, :], a1_send.at[d - 1], a1_recv.at[z], i, t,
        ).start()

    cols = tokens[:, pl.ds(pl.multiple_of(t * band, band), band)]
    pin = jnp.concatenate(
        [jnp.dot(cols, proj_in[k], preferred_element_type=F32) for k in range(2)], axis=1
    ).T
    for q in range(NT):
        for k in range(2):
            lo = k * rank + q * (rank // NT)
            pin_send[q, k] = pin[lo : lo + rank // NT]
    peers(lambda q: remote(pin_send.at[q], pin_recv.at[t], ps_send, ps_recv, z, q).start())

    for p in dests:
        drain(tok.at[p, my_rows, :], a1_recv.at[p])
        peers(
            lambda q: remote(
                tok.at[p, my_rows, :], tok.at[p, my_rows, :], a2_send.at[p], a2_recv.at[p], z, q
            ).start()
        )
    cg.wait()
    cu.wait()

    def forward(p, x):
        def tile(c, carry):
            at = pl.ds(pl.multiple_of(c * TILE, TILE), TILE)
            acc[p, 0, :, at] = jnp.dot(x(), wg[:, at], preferred_element_type=F32)
            acc[p, 1, :, at] = jnp.dot(x(), wu[:, at], preferred_element_type=F32)
            return carry

        lax.fori_loop(0, hid // TILE, tile, 0)

    def at_round(r):
        return pl.ds(pl.multiple_of(r * ROUND, ROUND), ROUND)

    def reduce(k, r):
        p, sl = dests[k], at_round(r)

        @pl.when(mid)
        def _():
            drain(recv.at[p, :, sl, :], red_recv.at[p, r])
            part[k, :, sl, :] = (acc[p, :, sl, :] + recv[p, :, sl, :].astype(F32)).astype(BF16)

        @pl.when(edge)
        def _():
            part[k, :, sl, :] = acc[p, :, sl, :].astype(BF16)

        remote(
            part.at[k, :, sl, :], recv.at[slots[k], :, sl, :],
            red_send.at[k, r], red_recv.at[slots[k], r], z + ways[k], t,
        ).start()

    def bcast(p, r, ssem, dz):
        sl = at_round(r)
        remote(dval.at[p, :, sl, :], dval.at[p, :, sl, :], ssem, bc_recv.at[p, r], dz, t).start()

    def root(r):
        sl = at_round(r)

        @pl.when(z > 0)
        def _():
            drain(recv.at[z, :, sl, :], red_recv.at[z, r])
            acc[z, :, sl, :] = acc[z, :, sl, :] + recv[z, :, sl, :].astype(F32)

        @pl.when(z < NDP - 1)
        def _():
            drain(recv.at[4, :, sl, :], red_recv.at[4, r])
            acc[z, :, sl, :] = acc[z, :, sl, :] + recv[4, :, sl, :].astype(F32)

        gate, up = acc[z, 0, sl, :], acc[z, 1, sl, :]
        cotan = hidden[sl, :].astype(F32)
        sigm = jax.nn.sigmoid(gate)
        dval[z, 0, sl, :] = (cotan * up * sigm * (1.0 + gate * (1.0 - sigm))).astype(BF16)
        dval[z, 1, sl, :] = (cotan * gate * sigm).astype(BF16)

        @pl.when(z < NDP - 1)
        def _():
            bcast(z, r, root_send.at[0, r], z + 1)

        @pl.when(z > 0)
        def _():
            bcast(z, r, root_send.at[1, r], z - 1)

    def onward(r):
        for k in (2, 1, 0):
            p = dests[k]
            drain(dval.at[p, :, at_round(r), :], bc_recv.at[p, r])

            @pl.when(mid)
            def _():
                bcast(p, r, fwd_send.at[k, r], z - ways[k])

    def at_block(b):
        return pl.ds(pl.multiple_of(b * brows, brows), brows)

    def backward(b):
        sl = at_block(b)
        per = band // TILE

        def tile(c, carry):
            at = pl.ds(pl.multiple_of(c * TILE, TILE), TILE)
            nt = (((1,), (1,)), ((), ()))
            dg = jnp.concatenate([dval[p, 0, sl, :] for p in range(NDP)], axis=0)
            du = jnp.concatenate([dval[p, 1, sl, :] for p in range(NDP)], axis=0)
            out = lax.dot_general(dg, wg[at, :], nt, preferred_element_type=F32)
            out = out + lax.dot_general(du, wu[at, :], nt, preferred_element_type=F32)
            out = out.astype(BF16)
            to = pl.ds(pl.multiple_of((c % per) * TILE, TILE), TILE)
            for p in range(NDP):
                term[2 * p + c // per, sl, to] = out[p * brows : (p + 1) * brows]
            return carry

        lax.fori_loop(0, block // TILE, tile, 0)
        peers(
            lambda q: remote(
                term.at[q, sl, :], landed.at[t, sl, :], rs_send.at[b], rs_recv.at[b], z, q
            ).start()
        )

    def finish(b):
        sl = at_block(b)
        drain(landed.at[pl.ds(0, NT - 1), sl, :], rs_recv.at[b])
        landed[t, sl, :] = term[t, sl, :]
        total = landed[0, sl, :].astype(F32)
        for j in range(1, NT):
            total = total + landed[j, sl, :].astype(F32)
        fin[sl, :] = total.astype(BF16)

        @pl.when(away)
        def _():
            remote(
                fin.at[sl, :], fin_land.at[sl, :], fin_send.at[b], fin_recv.at[b], pz, pt
            ).start()

    def features():
        for k in range(2):
            pg = jnp.dot(dval[z, k], proj_out[k], preferred_element_type=F32)
            pin_k = jnp.concatenate([pin_all[q, k] for q in range(NT)], axis=0)
            prod = jnp.dot(pin_k, pg, preferred_element_type=F32, precision=lax.Precision.HIGHEST)
            prod = jnp.concatenate([prod, jnp.zeros_like(prod)], axis=1)
            for q in range(NT):
                feat_send[q, k] = prod[q * (rank // NT) : (q + 1) * (rank // NT)]
        peers(lambda q: remote(feat_send.at[q], feat_recv.at[t], ft_send, ft_recv, z, q).start())

    own = pl.ds(pl.multiple_of(z * block, block), block)
    forward(z, lambda: tokens[:, own])

    drain(pin_recv.at[pl.ds(0, NT - 1)], ps_recv)
    pin_recv[t] = pin_send[t]
    total = pin_recv[0]
    for j in range(1, NT):
        total = total + pin_recv[j]
    pin_all[t] = total
    peers(lambda q: remote(pin_all.at[t], pin_all.at[t], pa_send, pa_recv, z, q).start())

    for k in range(3):
        p = dests[k]
        drain(tok.at[p, pl.ds(0, rows - share), :], a2_recv.at[p])
        forward(p, lambda: tok[p])
        reduce(k, 0)
    drain(pin_all.at[pl.ds(0, NT - 1)], pa_recv)

    def step(s, carry):
        @pl.when(s + 1 < rounds)
        def _():
            for k in range(3):
                reduce(k, s + 1)

        @pl.when(s < rounds)
        def _():
            root(s)

        @pl.when(s >= 1)
        def _():
            onward(s - 1)

        @pl.when(s == rounds - 1)
        def _():
            features()

        @pl.when(jnp.logical_and(s >= 2, s % 2 == 0))
        def _():
            backward(s // 2 - 1)

        @pl.when(jnp.logical_and(s >= 4, s % 2 == 0))
        def _():
            finish(s // 2 - 2)

        return carry

    lax.fori_loop(0, rounds + 1, step, 0)
    blocks = rounds // 2
    finish(blocks - 1)

    drain(feat_recv.at[pl.ds(0, NT - 1)], ft_recv)
    feat_recv[t] = feat_send[t]
    total = feat_recv[0]
    for j in range(1, NT):
        total = total + feat_recv[j]
    feat_out[0] = total[:, :, :rank]

    @pl.when(away)
    def _():
        def land(b, c):
            drain(fin_land.at[at_block(b), :], fin_recv.at[b])
            drain(fin.at[at_block(b), :], fin_send.at[b])
            return c

        lax.fori_loop(0, blocks, land, 0)
        grad_out[...] = fin_land[...]

    @pl.when(jnp.logical_not(away))
    def _():
        grad_out[...] = fin[...]

    for d in range(NDP - 1):
        drain(tok.at[0, my_rows, :], a1_send.at[d])
    for p in dests:
        drain(tok.at[0, pl.ds(0, rows - share), :], a2_send.at[p])
    drain(pin_send.at[pl.ds(0, NT - 1)], ps_send)
    drain(pin_all.at[pl.ds(0, NT - 1)], pa_send)
    drain(feat_send.at[pl.ds(0, NT - 1)], ft_send)

    def left(r, c):
        sl = at_round(r)
        for k in range(3):
            drain(part.at[k, :, sl, :], red_send.at[k, r])

            @pl.when(mid)
            def _():
                drain(part.at[k, :, sl, :], fwd_send.at[k, r])

        @pl.when(z < NDP - 1)
        def _():
            drain(part.at[0, :, sl, :], root_send.at[0, r])

        @pl.when(z > 0)
        def _():
            drain(part.at[0, :, sl, :], root_send.at[1, r])

        return c

    lax.fori_loop(0, rounds, left, 0)

    def left_rs(b, c):
        drain(term.at[pl.ds(0, NT - 1), at_block(b), :], rs_send.at[b])
        return c

    lax.fori_loop(0, blocks, left_rs, 0)


def fused_call(tokens, hidden_grad, gate_weight, up_weight, proj_in, proj_out):
    rows, width = tokens.shape
    block, hid = gate_weight.shape
    rank = proj_in.shape[2]
    band = width // NT
    rounds = rows // ROUND
    dma = pltpu.SemaphoreType.DMA
    vmem = pl.BlockSpec(memory_space=pltpu.VMEM)
    hbm = pl.BlockSpec(memory_space=pl.ANY)
    small = pltpu.VMEM((NT, 2, rank // NT, 128), F32)
    wide = (2, rows, hid)
    return pl.pallas_call(
        fused,
        out_shape=(
            jax.ShapeDtypeStruct((rows, band), BF16),
            jax.ShapeDtypeStruct((1, 2, rank // NT, rank), F32),
        ),
        in_specs=[vmem, vmem, hbm, hbm, vmem, vmem],
        out_specs=(vmem, vmem),
        scratch_shapes=[
            pltpu.VMEM((block, hid), BF16),
            pltpu.VMEM((block, hid), BF16),
            pltpu.VMEM((NDP, rows, block), BF16),
            pltpu.VMEM((NDP,) + wide, F32),
            pltpu.VMEM((3,) + wide, BF16),
            pltpu.VMEM((5,) + wide, BF16),
            pltpu.VMEM((NDP,) + wide, BF16),
            pltpu.VMEM((NT, rows, band), BF16),
            pltpu.VMEM((NT, rows, band), BF16),
            pltpu.VMEM((rows, band), BF16),
            pltpu.VMEM((rows, band), BF16),
            small, small, small, small, small,
            dma((2,)), dma((3,)), dma((NDP,)), dma((NDP,)), dma((NDP,)),
            dma((3, rounds)), dma((5, rounds)), dma((2, rounds)), dma((3, rounds)),
            dma((NDP, rounds)), dma((rounds // 2,)), dma((rounds // 2,)),
            dma((rounds // 2,)), dma((rounds // 2,)),
            dma(()), dma(()), dma(()), dma(()), dma(()), dma(()),
        ],
        compiler_params=pltpu.CompilerParams(
            collective_id=0, has_side_effects=True, vmem_limit_bytes=60 * 2**20
        ),
        cost_estimate=pl.CostEstimate(
            flops=16 * rows * NDP * block * hid // 2, bytes_accessed=8 * block * hid, transcendentals=rows * hid
        ),
    )(tokens, hidden_grad, gate_weight, up_weight, proj_in, proj_out)


def fits(mesh, tokens, gate_weight, proj_in):
    n_dp, n_tensor = mesh.shape["dp"], mesh.shape["tensor"]
    rows, width = tokens.shape[0] // n_dp, tokens.shape[1]
    hid = gate_weight.shape[1] // n_tensor
    return (
        (n_dp, n_tensor) == (NDP, NT)
        and rows == SEQ_LEN
        and width % (NT * TILE) == 0
        and hid % TILE == 0
        and proj_in.shape[2] == 64
    )


def solution(mesh):
    placed = (
        P("dp", None),
        P("dp", "tensor"),
        P("dp", "tensor"),
        P("dp", "tensor"),
        P(None, "tensor", None),
        P(None, "tensor", None),
    )

    def program(*args):
        if fits(mesh, args[0], args[2], args[4]):
            body = fused_call
        else:
            body = functools.partial(shards, mesh.shape["dp"], mesh.shape["tensor"])
        return jax.shard_map(
            body,
            mesh=mesh,
            in_specs=placed,
            out_specs=(P("dp", "tensor"), P("dp", None, "tensor", None)),
            check_vma=False,
        )(*args)

    return program
```

```python
import functools

import jax
import jax.numpy as jnp
from jax import lax
from jax.experimental import pallas as pl
from jax.experimental.pallas import tpu as pltpu
from jax.sharding import PartitionSpec as P

SEQ_LEN = 128
F32 = jnp.float32
BF16 = jnp.bfloat16


def shards(n_dp, n_tensor, tokens, hidden_grad, gate_weight, up_weight, proj_in, proj_out):
    highest = lax.Precision.HIGHEST
    place = lax.axis_index("tensor")
    rows, width = tokens.shape
    rank = proj_in.shape[2]
    block = width // n_dp
    band = width // n_tensor
    halves = n_tensor // n_dp
    share = rows // n_tensor

    mine = lax.dynamic_slice_in_dim(tokens, place * share, share, 0)
    mine = mine.reshape(share, n_dp, block).transpose(1, 0, 2)
    mine = lax.all_to_all(mine, "dp", 0, 0)
    tok = lax.all_gather(mine, "tensor", axis=1, tiled=True).reshape(n_dp * rows, block)

    gate_part = jnp.dot(tok, gate_weight, preferred_element_type=F32).astype(BF16)
    up_part = jnp.dot(tok, up_weight, preferred_element_type=F32).astype(BF16)
    gate = lax.psum_scatter(gate_part, "dp", scatter_dimension=0, tiled=True).astype(F32)
    up = lax.psum_scatter(up_part, "dp", scatter_dimension=0, tiled=True).astype(F32)
    cotan = hidden_grad.astype(F32)
    sigm = jax.nn.sigmoid(gate)
    d_gate = (cotan * up * sigm * (1.0 + gate * (1.0 - sigm))).astype(BF16)
    d_up = (cotan * gate * sigm).astype(BF16)
    d_gate_all = lax.all_gather(d_gate, "dp", axis=0, tiled=True)
    d_up_all = lax.all_gather(d_up, "dp", axis=0, tiled=True)
    term = jnp.einsum("tf,df->td", d_gate_all, gate_weight, preferred_element_type=F32)
    term = (term + jnp.einsum("tf,df->td", d_up_all, up_weight, preferred_element_type=F32)).astype(BF16)
    term = term.reshape(n_dp, rows, halves, band).transpose(0, 2, 1, 3).reshape(n_tensor * rows, band)
    piece = lax.psum_scatter(term, "tensor", scatter_dimension=0, tiled=True)
    pairs = []
    for i in range(n_dp):
        for m in range(n_tensor):
            p, h = divmod(m, halves)
            pairs.append((i * n_tensor + m, p * n_tensor + i * halves + h))
    input_grad = lax.ppermute(piece, ("dp", "tensor"), pairs)

    local_cols = lax.dynamic_slice_in_dim(tokens, place * band, band, 1)
    in_partial = jnp.einsum("td,kda->tka", local_cols, proj_in, preferred_element_type=F32)
    projected_in = lax.psum(in_partial, "tensor")
    grad_partial = jnp.stack(
        [
            jnp.dot(d_gate, proj_out[0], preferred_element_type=F32),
            jnp.dot(d_up, proj_out[1], preferred_element_type=F32),
        ],
        axis=1,
    )
    seqs = rows // SEQ_LEN
    seq_in = projected_in.reshape(seqs, SEQ_LEN, 2, rank)
    seq_grad = grad_partial.reshape(seqs, SEQ_LEN, 2, rank)
    terms = jnp.einsum("slka,slkb->skab", seq_in, seq_grad, precision=highest)
    features = lax.psum_scatter(terms, "tensor", scatter_dimension=2, tiled=True)
    return (input_grad, features)


ROUND = 16
TILE = 256
NDP = 4
NT = 8


def fused(
    tokens, hidden, gate_hbm, up_hbm, proj_in, proj_out, grad_out, feat_out,
    wg, wu, tok, acc, part, recv, dval, term, landed, fin, fin_land,
    pin_send, pin_recv, pin_all, feat_send, feat_recv,
    w_sem, a1_send, a1_recv, a2_send, a2_recv, a3_send, a3_recv, red_send, red_recv,
    root_send, fwd_send, bc_recv, rs_send, rs_recv, fin_send, fin_recv,
    ps_send, ps_recv, pa_send, pa_recv, ft_send, ft_recv,
):
    z, t = lax.axis_index("dp"), lax.axis_index("tensor")
    rows, width = tokens.shape
    block, hid = wg.shape
    band = width // NT
    rank = proj_in.shape[2]
    share = rows // NT
    rounds = rows // ROUND
    brows = 2 * ROUND
    mid = jnp.logical_and(z > 0, z < NDP - 1)
    edge = jnp.logical_or(z == 0, z == NDP - 1)
    low = z // 2
    o0 = 3 - 3 * low
    o2 = z + 1 - 2 * low
    o1 = 6 - z - o0 - o2
    ways = (1 - 2 * low, 1 - 2 * (z % 2), 1 - 2 * low)
    dests = (o0, o1, o2)
    is1 = (z % 2) * (1 - low)
    slots = (o0, o1 + (4 - o1) * is1, o2 + (4 - o2) * low)
    pz, pt = t // 2, 2 * z + t % 2
    away = pz != z

    def remote(src, dst, ssem, rsem, dz, dt):
        return pltpu.make_async_remote_copy(
            src_ref=src, dst_ref=dst, send_sem=ssem, recv_sem=rsem,
            device_id=(dz, dt), device_id_type=pl.DeviceIdType.MESH,
        )

    def drain(ref, sem):
        pltpu.make_async_copy(ref, ref, sem).wait()

    def peers(fn):
        def step(d, c):
            fn(lax.rem(t + d, NT))
            return c

        lax.fori_loop(1, NT, step, 0)

    cg = pltpu.make_async_copy(gate_hbm, wg, w_sem.at[0])
    cu = pltpu.make_async_copy(up_hbm, wu, w_sem.at[1])
    cg.start()
    cu.start()

    barrier = pltpu.get_barrier_semaphore()

    def hello(dz, dt):
        pl.semaphore_signal(barrier, inc=1, device_id=(dz, dt), device_id_type=pl.DeviceIdType.MESH)

    peers(lambda q: hello(z, q))
    for d in range(1, NDP):
        hello(lax.rem(z + d, NDP), t)

    @pl.when(away)
    def _():
        hello(pz, pt)
        pl.semaphore_wait(barrier, NT + NDP - 1)

    @pl.when(jnp.logical_not(away))
    def _():
        pl.semaphore_wait(barrier, NT + NDP - 2)

    my_rows = pl.ds(pl.multiple_of(t * share, share), share)
    for d in range(1, NDP):
        i = lax.rem(z + d, NDP)
        remote(
            tokens.at[my_rows, pl.ds(pl.multiple_of(i * block, block), block)],
            tok.at[z, my_rows, :], a1_send.at[d - 1], a1_recv.at[z], i, t,
        ).start()

    cols = tokens[:, pl.ds(pl.multiple_of(t * band, band), band)]
    pin = jnp.concatenate(
        [jnp.dot(cols, proj_in[k], preferred_element_type=F32) for k in range(2)], axis=1
    ).T
    for q in range(NT):
        for k in range(2):
            lo = k * rank + q * (rank // NT)
            pin_send[q, k] = pin[lo : lo + rank // NT]
    peers(lambda q: remote(pin_send.at[q], pin_recv.at[t], ps_send, ps_recv, z, q).start())

    for p in dests:
        drain(tok.at[p, my_rows, :], a1_recv.at[p])
        for d in range(1, NT // 2):
            remote(
                tok.at[p, my_rows, :], tok.at[p, my_rows, :],
                a2_send.at[p], a2_recv.at[p], z, lax.rem(t + 2 * d, NT),
            ).start()
    for p in dests:
        drain(tok.at[p, pl.ds(0, 3 * share), :], a2_recv.at[p])
        for d in range(NT // 2):
            q_rows = pl.ds(pl.multiple_of(lax.rem(t + 2 * d, NT) * share, share), share)
            remote(
                tok.at[p, q_rows, :], tok.at[p, q_rows, :],
                a3_send.at[p], a3_recv.at[p], z, t + 1 - 2 * (t % 2),
            ).start()
    cg.wait()
    cu.wait()

    def forward(p, x):
        def tile(c, carry):
            at = pl.ds(pl.multiple_of(c * TILE, TILE), TILE)
            acc[p, 0, :, at] = jnp.dot(x(), wg[:, at], preferred_element_type=F32)
            acc[p, 1, :, at] = jnp.dot(x(), wu[:, at], preferred_element_type=F32)
            return carry

        lax.fori_loop(0, hid // TILE, tile, 0)

    def at_round(r):
        return pl.ds(pl.multiple_of(r * ROUND, ROUND), ROUND)

    def reduce(k, r):
        p, sl = dests[k], at_round(r)

        @pl.when(mid)
        def _():
            drain(recv.at[p, :, sl, :], red_recv.at[p, r])
            part[k, :, sl, :] = (acc[p, :, sl, :] + recv[p, :, sl, :].astype(F32)).astype(BF16)

        @pl.when(edge)
        def _():
            part[k, :, sl, :] = acc[p, :, sl, :].astype(BF16)

        remote(
            part.at[k, :, sl, :], recv.at[slots[k], :, sl, :],
            red_send.at[k, r], red_recv.at[slots[k], r], z + ways[k], t,
        ).start()

    def bcast(p, r, ssem, dz):
        sl = at_round(r)
        remote(dval.at[p, :, sl, :], dval.at[p, :, sl, :], ssem, bc_recv.at[p, r], dz, t).start()

    def root(r):
        sl = at_round(r)

        @pl.when(z > 0)
        def _():
            drain(recv.at[z, :, sl, :], red_recv.at[z, r])
            acc[z, :, sl, :] = acc[z, :, sl, :] + recv[z, :, sl, :].astype(F32)

        @pl.when(z < NDP - 1)
        def _():
            drain(recv.at[4, :, sl, :], red_recv.at[4, r])
            acc[z, :, sl, :] = acc[z, :, sl, :] + recv[4, :, sl, :].astype(F32)

        gate, up = acc[z, 0, sl, :], acc[z, 1, sl, :]
        cotan = hidden[sl, :].astype(F32)
        sigm = jax.nn.sigmoid(gate)
        dval[z, 0, sl, :] = (cotan * up * sigm * (1.0 + gate * (1.0 - sigm))).astype(BF16)
        dval[z, 1, sl, :] = (cotan * gate * sigm).astype(BF16)

        @pl.when(z < NDP - 1)
        def _():
            bcast(z, r, root_send.at[0, r], z + 1)

        @pl.when(z > 0)
        def _():
            bcast(z, r, root_send.at[1, r], z - 1)

    def onward(k, r):
        p = dests[k]
        drain(dval.at[p, :, at_round(r), :], bc_recv.at[p, r])

        @pl.when(mid)
        def _():
            bcast(p, r, fwd_send.at[k, r], z - ways[k])

    def at_block(b):
        return pl.ds(pl.multiple_of(b * brows, brows), brows)

    def backward(b):
        sl = at_block(b)
        per = band // TILE

        def tile(c, carry):
            at = pl.ds(pl.multiple_of(c * TILE, TILE), TILE)
            nt = (((1,), (1,)), ((), ()))
            dg = jnp.concatenate([dval[p, 0, sl, :] for p in range(NDP)], axis=0)
            du = jnp.concatenate([dval[p, 1, sl, :] for p in range(NDP)], axis=0)
            out = lax.dot_general(dg, wg[at, :], nt, preferred_element_type=F32)
            out = out + lax.dot_general(du, wu[at, :], nt, preferred_element_type=F32)
            out = out.astype(BF16)
            to = pl.ds(pl.multiple_of((c % per) * TILE, TILE), TILE)
            for p in range(NDP):
                term[2 * p + c // per, sl, to] = out[p * brows : (p + 1) * brows]
            return carry

        lax.fori_loop(0, block // TILE, tile, 0)
        peers(
            lambda q: remote(
                term.at[q, sl, :], landed.at[t, sl, :], rs_send.at[b], rs_recv.at[b], z, q
            ).start()
        )

    def finish(b):
        sl = at_block(b)
        drain(landed.at[pl.ds(0, NT - 1), sl, :], rs_recv.at[b])
        landed[t, sl, :] = term[t, sl, :]
        total = landed[0, sl, :].astype(F32)
        for j in range(1, NT):
            total = total + landed[j, sl, :].astype(F32)
        fin[sl, :] = total.astype(BF16)

        @pl.when(away)
        def _():
            remote(
                fin.at[sl, :], fin_land.at[sl, :], fin_send.at[b], fin_recv.at[b], pz, pt
            ).start()

    def features():
        for k in range(2):
            pg = jnp.dot(dval[z, k], proj_out[k], preferred_element_type=F32)
            pin_k = jnp.concatenate([pin_all[q, k] for q in range(NT)], axis=0)
            prod = jnp.dot(pin_k, pg, preferred_element_type=F32, precision=lax.Precision.HIGHEST)
            prod = jnp.concatenate([prod, jnp.zeros_like(prod)], axis=1)
            for q in range(NT):
                feat_send[q, k] = prod[q * (rank // NT) : (q + 1) * (rank // NT)]
        peers(lambda q: remote(feat_send.at[q], feat_recv.at[t], ft_send, ft_recv, z, q).start())

    own = pl.ds(pl.multiple_of(z * block, block), block)
    forward(z, lambda: tokens[:, own])

    drain(pin_recv.at[pl.ds(0, NT - 1)], ps_recv)
    pin_recv[t] = pin_send[t]
    total = pin_recv[0]
    for j in range(1, NT):
        total = total + pin_recv[j]
    pin_all[t] = total
    peers(lambda q: remote(pin_all.at[t], pin_all.at[t], pa_send, pa_recv, z, q).start())

    for k in range(3):
        p = dests[k]
        drain(tok.at[p, pl.ds(0, rows // 2), :], a3_recv.at[p])
        forward(p, lambda: tok[p])
    drain(pin_all.at[pl.ds(0, NT - 1)], pa_recv)

    def inner(p):
        return (p % 2) * (1 - p // 2) + (p // 2) * (1 - p % 2)

    ups = (1 - low, 1 - z % 2, 1 - low)
    hops = tuple(z * u + (NDP - 1 - z) * (1 - u) for u in ups)
    root_lag = 3 - inner(z)
    on_lags = tuple(3 - inner(p) + w * (p - z) for p, w in zip(dests, ways))
    last_lag = 6 - inner(z)

    def within(r):
        return jnp.logical_and(r >= 0, r < rounds)

    def step(s, carry):
        for k in range(3):

            @pl.when(within(s - hops[k]))
            def _():
                reduce(k, s - hops[k])

        @pl.when(within(s - root_lag))
        def _():
            root(s - root_lag)

        for k in (2, 1, 0):

            @pl.when(within(s - on_lags[k]))
            def _():
                onward(k, s - on_lags[k])

        @pl.when(s - root_lag == rounds - 1)
        def _():
            features()

        done = s - last_lag + 1

        @pl.when(jnp.logical_and(within(done - 1), done % 2 == 0))
        def _():
            backward(done // 2 - 1)

            @pl.when(done >= 4)
            def _():
                finish(done // 2 - 2)

        return carry

    lax.fori_loop(0, rounds + 6, step, 0)
    blocks = rounds // 2
    finish(blocks - 1)

    drain(feat_recv.at[pl.ds(0, NT - 1)], ft_recv)
    feat_recv[t] = feat_send[t]
    total = feat_recv[0]
    for j in range(1, NT):
        total = total + feat_recv[j]
    feat_out[0] = total[:, :, :rank]

    @pl.when(away)
    def _():
        def land(b, c):
            drain(fin_land.at[at_block(b), :], fin_recv.at[b])
            drain(fin.at[at_block(b), :], fin_send.at[b])
            return c

        lax.fori_loop(0, blocks, land, 0)
        grad_out[...] = fin_land[...]

    @pl.when(jnp.logical_not(away))
    def _():
        grad_out[...] = fin[...]

    for d in range(NDP - 1):
        drain(tok.at[0, my_rows, :], a1_send.at[d])
    for p in dests:
        drain(tok.at[0, pl.ds(0, 3 * share), :], a2_send.at[p])
        drain(tok.at[0, pl.ds(0, rows // 2), :], a3_send.at[p])
    drain(pin_send.at[pl.ds(0, NT - 1)], ps_send)
    drain(pin_all.at[pl.ds(0, NT - 1)], pa_send)
    drain(feat_send.at[pl.ds(0, NT - 1)], ft_send)

    def left(r, c):
        sl = at_round(r)
        for k in range(3):
            drain(part.at[k, :, sl, :], red_send.at[k, r])

            @pl.when(mid)
            def _():
                drain(part.at[k, :, sl, :], fwd_send.at[k, r])

        @pl.when(z < NDP - 1)
        def _():
            drain(part.at[0, :, sl, :], root_send.at[0, r])

        @pl.when(z > 0)
        def _():
            drain(part.at[0, :, sl, :], root_send.at[1, r])

        return c

    lax.fori_loop(0, rounds, left, 0)

    def left_rs(b, c):
        drain(term.at[pl.ds(0, NT - 1), at_block(b), :], rs_send.at[b])
        return c

    lax.fori_loop(0, blocks, left_rs, 0)


def fused_call(tokens, hidden_grad, gate_weight, up_weight, proj_in, proj_out):
    rows, width = tokens.shape
    block, hid = gate_weight.shape
    rank = proj_in.shape[2]
    band = width // NT
    rounds = rows // ROUND
    dma = pltpu.SemaphoreType.DMA
    vmem = pl.BlockSpec(memory_space=pltpu.VMEM)
    hbm = pl.BlockSpec(memory_space=pl.ANY)
    small = pltpu.VMEM((NT, 2, rank // NT, 128), F32)
    wide = (2, rows, hid)
    return pl.pallas_call(
        fused,
        out_shape=(
            jax.ShapeDtypeStruct((rows, band), BF16),
            jax.ShapeDtypeStruct((1, 2, rank // NT, rank), F32),
        ),
        in_specs=[vmem, vmem, hbm, hbm, vmem, vmem],
        out_specs=(vmem, vmem),
        scratch_shapes=[
            pltpu.VMEM((block, hid), BF16),
            pltpu.VMEM((block, hid), BF16),
            pltpu.VMEM((NDP, rows, block), BF16),
            pltpu.VMEM((NDP,) + wide, F32),
            pltpu.VMEM((3,) + wide, BF16),
            pltpu.VMEM((5,) + wide, BF16),
            pltpu.VMEM((NDP,) + wide, BF16),
            pltpu.VMEM((NT, rows, band), BF16),
            pltpu.VMEM((NT, rows, band), BF16),
            pltpu.VMEM((rows, band), BF16),
            pltpu.VMEM((rows, band), BF16),
            small, small, small, small, small,
            dma((2,)), dma((3,)), dma((NDP,)), dma((NDP,)), dma((NDP,)), dma((NDP,)), dma((NDP,)),
            dma((3, rounds)), dma((5, rounds)), dma((2, rounds)), dma((3, rounds)),
            dma((NDP, rounds)), dma((rounds // 2,)), dma((rounds // 2,)),
            dma((rounds // 2,)), dma((rounds // 2,)),
            dma(()), dma(()), dma(()), dma(()), dma(()), dma(()),
        ],
        compiler_params=pltpu.CompilerParams(
            collective_id=0, has_side_effects=True, vmem_limit_bytes=60 * 2**20
        ),
        cost_estimate=pl.CostEstimate(
            flops=16 * rows * NDP * block * hid // 2, bytes_accessed=8 * block * hid, transcendentals=rows * hid
        ),
    )(tokens, hidden_grad, gate_weight, up_weight, proj_in, proj_out)


def fits(mesh, tokens, gate_weight, proj_in):
    n_dp, n_tensor = mesh.shape["dp"], mesh.shape["tensor"]
    rows, width = tokens.shape[0] // n_dp, tokens.shape[1]
    hid = gate_weight.shape[1] // n_tensor
    return (
        (n_dp, n_tensor) == (NDP, NT)
        and rows == SEQ_LEN
        and width % (NT * TILE) == 0
        and hid % TILE == 0
        and proj_in.shape[2] == 64
    )


def solution(mesh):
    placed = (
        P("dp", None),
        P("dp", "tensor"),
        P("dp", "tensor"),
        P("dp", "tensor"),
        P(None, "tensor", None),
        P(None, "tensor", None),
    )

    def program(*args):
        if fits(mesh, args[0], args[2], args[4]):
            body = fused_call
        else:
            body = functools.partial(shards, mesh.shape["dp"], mesh.shape["tensor"])
        return jax.shard_map(
            body,
            mesh=mesh,
            in_specs=placed,
            out_specs=(P("dp", "tensor"), P("dp", None, "tensor", None)),
            check_vma=False,
        )(*args)

    return program
```

```python
import functools

import jax
import jax.numpy as jnp
from jax import lax
from jax.experimental import pallas as pl
from jax.experimental.pallas import tpu as pltpu
from jax.sharding import PartitionSpec as P

SEQ_LEN = 128
F32 = jnp.float32
BF16 = jnp.bfloat16


def shards(n_dp, n_tensor, tokens, hidden_grad, gate_weight, up_weight, proj_in, proj_out):
    highest = lax.Precision.HIGHEST
    place = lax.axis_index("tensor")
    rows, width = tokens.shape
    rank = proj_in.shape[2]
    block = width // n_dp
    band = width // n_tensor
    halves = n_tensor // n_dp
    share = rows // n_tensor

    mine = lax.dynamic_slice_in_dim(tokens, place * share, share, 0)
    mine = mine.reshape(share, n_dp, block).transpose(1, 0, 2)
    mine = lax.all_to_all(mine, "dp", 0, 0)
    tok = lax.all_gather(mine, "tensor", axis=1, tiled=True).reshape(n_dp * rows, block)

    gate_part = jnp.dot(tok, gate_weight, preferred_element_type=F32).astype(BF16)
    up_part = jnp.dot(tok, up_weight, preferred_element_type=F32).astype(BF16)
    gate = lax.psum_scatter(gate_part, "dp", scatter_dimension=0, tiled=True).astype(F32)
    up = lax.psum_scatter(up_part, "dp", scatter_dimension=0, tiled=True).astype(F32)
    cotan = hidden_grad.astype(F32)
    sigm = jax.nn.sigmoid(gate)
    d_gate = (cotan * up * sigm * (1.0 + gate * (1.0 - sigm))).astype(BF16)
    d_up = (cotan * gate * sigm).astype(BF16)
    d_gate_all = lax.all_gather(d_gate, "dp", axis=0, tiled=True)
    d_up_all = lax.all_gather(d_up, "dp", axis=0, tiled=True)
    term = jnp.einsum("tf,df->td", d_gate_all, gate_weight, preferred_element_type=F32)
    term = (term + jnp.einsum("tf,df->td", d_up_all, up_weight, preferred_element_type=F32)).astype(BF16)
    term = term.reshape(n_dp, rows, halves, band).transpose(0, 2, 1, 3).reshape(n_tensor * rows, band)
    piece = lax.psum_scatter(term, "tensor", scatter_dimension=0, tiled=True)
    pairs = []
    for i in range(n_dp):
        for m in range(n_tensor):
            p, h = divmod(m, halves)
            pairs.append((i * n_tensor + m, p * n_tensor + i * halves + h))
    input_grad = lax.ppermute(piece, ("dp", "tensor"), pairs)

    local_cols = lax.dynamic_slice_in_dim(tokens, place * band, band, 1)
    in_partial = jnp.einsum("td,kda->tka", local_cols, proj_in, preferred_element_type=F32)
    projected_in = lax.psum(in_partial, "tensor")
    grad_partial = jnp.stack(
        [
            jnp.dot(d_gate, proj_out[0], preferred_element_type=F32),
            jnp.dot(d_up, proj_out[1], preferred_element_type=F32),
        ],
        axis=1,
    )
    seqs = rows // SEQ_LEN
    seq_in = projected_in.reshape(seqs, SEQ_LEN, 2, rank)
    seq_grad = grad_partial.reshape(seqs, SEQ_LEN, 2, rank)
    terms = jnp.einsum("slka,slkb->skab", seq_in, seq_grad, precision=highest)
    features = lax.psum_scatter(terms, "tensor", scatter_dimension=2, tiled=True)
    return (input_grad, features)


ROUND = 16
TILE = 256
NDP = 4
NT = 8


def fused(
    tokens, hidden, gate_hbm, up_hbm, proj_in, proj_out, grad_out, feat_out,
    wg, wu, tok, acc, part, recv, dval, term, landed, fin, fin_land,
    pin_send, pin_recv, pin_all, feat_send, feat_recv,
    w_sem, a1_send, a1_recv, a2_send, a2_recv, a3_send, a3_recv, red_send, red_recv,
    root_send, fwd_send, bc_recv, rs_send, rs_recv, fin_send, fin_recv,
    ps_send, ps_recv, pa_send, pa_recv, ft_send, ft_recv,
):
    z, t = lax.axis_index("dp"), lax.axis_index("tensor")
    rows, width = tokens.shape
    block, hid = wg.shape
    band = width // NT
    rank = proj_in.shape[2]
    share = rows // NT
    rounds = rows // ROUND
    brows = 2 * ROUND
    mid = jnp.logical_and(z > 0, z < NDP - 1)
    edge = jnp.logical_or(z == 0, z == NDP - 1)
    low = z // 2
    o0 = 3 - 3 * low
    o2 = z + 1 - 2 * low
    o1 = 6 - z - o0 - o2
    ways = (1 - 2 * low, 1 - 2 * (z % 2), 1 - 2 * low)
    dests = (o0, o1, o2)
    is1 = (z % 2) * (1 - low)
    slots = (o0, o1 + (4 - o1) * is1, o2 + (4 - o2) * low)
    pz, pt = t // 2, 2 * z + t % 2
    away = pz != z

    def remote(src, dst, ssem, rsem, dz, dt):
        return pltpu.make_async_remote_copy(
            src_ref=src, dst_ref=dst, send_sem=ssem, recv_sem=rsem,
            device_id=(dz, dt), device_id_type=pl.DeviceIdType.MESH,
        )

    def drain(ref, sem):
        pltpu.make_async_copy(ref, ref, sem).wait()

    def peers(fn):
        def step(d, c):
            fn(lax.rem(t + d, NT))
            return c

        lax.fori_loop(1, NT, step, 0)

    cg = pltpu.make_async_copy(gate_hbm, wg, w_sem.at[0])
    cu = pltpu.make_async_copy(up_hbm, wu, w_sem.at[1])
    cg.start()
    cu.start()

    barrier = pltpu.get_barrier_semaphore()

    def hello(dz, dt):
        pl.semaphore_signal(barrier, inc=1, device_id=(dz, dt), device_id_type=pl.DeviceIdType.MESH)

    peers(lambda q: hello(z, q))
    for d in range(1, NDP):
        hello(lax.rem(z + d, NDP), t)

    @pl.when(away)
    def _():
        hello(pz, pt)
        pl.semaphore_wait(barrier, NT + NDP - 1)

    @pl.when(jnp.logical_not(away))
    def _():
        pl.semaphore_wait(barrier, NT + NDP - 2)

    my_rows = pl.ds(pl.multiple_of(t * share, share), share)
    for d in range(1, NDP):
        i = lax.rem(z + d, NDP)
        remote(
            tokens.at[my_rows, pl.ds(pl.multiple_of(i * block, block), block)],
            tok.at[z, my_rows, :], a1_send.at[d - 1], a1_recv.at[z], i, t,
        ).start()

    cols = tokens[:, pl.ds(pl.multiple_of(t * band, band), band)]
    pin = jnp.concatenate(
        [jnp.dot(cols, proj_in[k], preferred_element_type=F32) for k in range(2)], axis=1
    ).T
    for q in range(NT):
        for k in range(2):
            lo = k * rank + q * (rank // NT)
            pin_send[q, k] = pin[lo : lo + rank // NT]
    peers(lambda q: remote(pin_send.at[q], pin_recv.at[t], ps_send, ps_recv, z, q).start())

    for p in dests:
        drain(tok.at[p, my_rows, :], a1_recv.at[p])
        for d in range(1, NT // 2):
            remote(
                tok.at[p, my_rows, :], tok.at[p, my_rows, :],
                a2_send.at[p], a2_recv.at[p], z, lax.rem(t + 2 * d, NT),
            ).start()
    for p in dests:
        drain(tok.at[p, pl.ds(0, 3 * share), :], a2_recv.at[p])
        for d in range(NT // 2):
            q_rows = pl.ds(pl.multiple_of(lax.rem(t + 2 * d, NT) * share, share), share)
            remote(
                tok.at[p, q_rows, :], tok.at[p, q_rows, :],
                a3_send.at[p], a3_recv.at[p], z, t + 1 - 2 * (t % 2),
            ).start()
    cg.wait()
    cu.wait()

    def forward(p, x):
        def tile(c, carry):
            at = pl.ds(pl.multiple_of(c * TILE, TILE), TILE)
            acc[p, 0, :, at] = jnp.dot(x(), wg[:, at], preferred_element_type=F32)
            acc[p, 1, :, at] = jnp.dot(x(), wu[:, at], preferred_element_type=F32)
            return carry

        lax.fori_loop(0, hid // TILE, tile, 0)

    def at_round(r):
        return pl.ds(pl.multiple_of(r * ROUND, ROUND), ROUND)

    def reduce(k, r):
        p, sl = dests[k], at_round(r)

        @pl.when(mid)
        def _():
            drain(recv.at[p, :, sl, :], red_recv.at[p, r])
            part[k, :, sl, :] = (acc[p, :, sl, :] + recv[p, :, sl, :].astype(F32)).astype(BF16)

        @pl.when(edge)
        def _():
            part[k, :, sl, :] = acc[p, :, sl, :].astype(BF16)

        remote(
            part.at[k, :, sl, :], recv.at[slots[k], :, sl, :],
            red_send.at[k, r], red_recv.at[slots[k], r], z + ways[k], t,
        ).start()

    def bcast(p, r, ssem, dz):
        sl = at_round(r)
        remote(dval.at[p, :, sl, :], dval.at[p, :, sl, :], ssem, bc_recv.at[p, r], dz, t).start()

    def root(r):
        sl = at_round(r)

        @pl.when(z > 0)
        def _():
            drain(recv.at[z, :, sl, :], red_recv.at[z, r])
            acc[z, :, sl, :] = acc[z, :, sl, :] + recv[z, :, sl, :].astype(F32)

        @pl.when(z < NDP - 1)
        def _():
            drain(recv.at[4, :, sl, :], red_recv.at[4, r])
            acc[z, :, sl, :] = acc[z, :, sl, :] + recv[4, :, sl, :].astype(F32)

        gate, up = acc[z, 0, sl, :], acc[z, 1, sl, :]
        cotan = hidden[sl, :].astype(F32)
        sigm = jax.nn.sigmoid(gate)
        dval[z, 0, sl, :] = (cotan * up * sigm * (1.0 + gate * (1.0 - sigm))).astype(BF16)
        dval[z, 1, sl, :] = (cotan * gate * sigm).astype(BF16)

        @pl.when(z < NDP - 1)
        def _():
            bcast(z, r, root_send.at[0, r], z + 1)

        @pl.when(z > 0)
        def _():
            bcast(z, r, root_send.at[1, r], z - 1)

    def onward(k, r):
        p = dests[k]
        drain(dval.at[p, :, at_round(r), :], bc_recv.at[p, r])

        @pl.when(mid)
        def _():
            bcast(p, r, fwd_send.at[k, r], z - ways[k])

    def at_block(b):
        return pl.ds(pl.multiple_of(b * brows, brows), brows)

    def backward(b):
        sl = at_block(b)
        per = band // TILE

        def tile(c, carry):
            at = pl.ds(pl.multiple_of(c * TILE, TILE), TILE)
            nt = (((1,), (1,)), ((), ()))
            dg = jnp.concatenate([dval[p, 0, sl, :] for p in range(NDP)], axis=0)
            du = jnp.concatenate([dval[p, 1, sl, :] for p in range(NDP)], axis=0)
            out = lax.dot_general(dg, wg[at, :], nt, preferred_element_type=F32)
            out = out + lax.dot_general(du, wu[at, :], nt, preferred_element_type=F32)
            out = out.astype(BF16)
            to = pl.ds(pl.multiple_of((c % per) * TILE, TILE), TILE)
            for p in range(NDP):
                term[2 * p + c // per, sl, to] = out[p * brows : (p + 1) * brows]
            return carry

        lax.fori_loop(0, block // TILE, tile, 0)
        peers(
            lambda q: remote(
                term.at[q, sl, :], landed.at[t, sl, :], rs_send.at[b], rs_recv.at[b], z, q
            ).start()
        )

    def finish(b):
        sl = at_block(b)
        drain(landed.at[pl.ds(0, NT - 1), sl, :], rs_recv.at[b])
        landed[t, sl, :] = term[t, sl, :]
        total = landed[0, sl, :].astype(F32)
        for j in range(1, NT):
            total = total + landed[j, sl, :].astype(F32)
        fin[sl, :] = total.astype(BF16)

        @pl.when(away)
        def _():
            remote(
                fin.at[sl, :], fin_land.at[sl, :], fin_send.at[b], fin_recv.at[b], pz, pt
            ).start()

    def features():
        for k in range(2):
            pg = jnp.dot(dval[z, k], proj_out[k], preferred_element_type=F32)
            pin_k = jnp.concatenate([pin_all[q, k] for q in range(NT)], axis=0)
            prod = jnp.dot(pin_k, pg, preferred_element_type=F32, precision=lax.Precision.HIGHEST)
            prod = jnp.concatenate([prod, jnp.zeros_like(prod)], axis=1)
            for q in range(NT):
                feat_send[q, k] = prod[q * (rank // NT) : (q + 1) * (rank // NT)]
        peers(lambda q: remote(feat_send.at[q], feat_recv.at[t], ft_send, ft_recv, z, q).start())

    own = pl.ds(pl.multiple_of(z * block, block), block)
    forward(z, lambda: tokens[:, own])

    drain(pin_recv.at[pl.ds(0, NT - 1)], ps_recv)
    pin_recv[t] = pin_send[t]
    total = pin_recv[0]
    for j in range(1, NT):
        total = total + pin_recv[j]
    pin_all[t] = total
    peers(lambda q: remote(pin_all.at[t], pin_all.at[t], pa_send, pa_recv, z, q).start())

    for k in range(3):
        p = dests[k]
        drain(tok.at[p, pl.ds(0, rows // 2), :], a3_recv.at[p])
        forward(p, lambda: tok[p])

        @pl.when(edge)
        def _():
            reduce(k, 0)

    drain(pin_all.at[pl.ds(0, NT - 1)], pa_recv)

    def inner(p):
        return (p % 2) * (1 - p // 2) + (p // 2) * (1 - p % 2)

    ups = (1 - low, 1 - z % 2, 1 - low)
    hops = tuple(z * u + (NDP - 1 - z) * (1 - u) for u in ups)
    root_lag = 3 - inner(z)
    on_lags = tuple(3 - inner(p) + w * (p - z) for p, w in zip(dests, ways))
    last_lag = 6 - inner(z)

    def within(r):
        return jnp.logical_and(r >= 0, r < rounds)

    def step(s, carry):
        for k in range(3):

            @pl.when(jnp.logical_and(within(s - hops[k]), jnp.logical_or(mid, s > 0)))
            def _():
                reduce(k, s - hops[k])

        @pl.when(within(s - root_lag))
        def _():
            root(s - root_lag)

        for k in (2, 1, 0):

            @pl.when(within(s - on_lags[k]))
            def _():
                onward(k, s - on_lags[k])

        @pl.when(s - root_lag == rounds - 1)
        def _():
            features()

        done = s - last_lag + 1

        @pl.when(jnp.logical_and(within(done - 1), done % 2 == 0))
        def _():
            backward(done // 2 - 1)

            @pl.when(done >= 4)
            def _():
                finish(done // 2 - 2)

        return carry

    lax.fori_loop(0, rounds + 6, step, 0)
    blocks = rounds // 2
    finish(blocks - 1)

    drain(feat_recv.at[pl.ds(0, NT - 1)], ft_recv)
    feat_recv[t] = feat_send[t]
    total = feat_recv[0]
    for j in range(1, NT):
        total = total + feat_recv[j]
    feat_out[0] = total[:, :, :rank]

    @pl.when(away)
    def _():
        def land(b, c):
            drain(fin_land.at[at_block(b), :], fin_recv.at[b])
            drain(fin.at[at_block(b), :], fin_send.at[b])
            return c

        lax.fori_loop(0, blocks, land, 0)
        grad_out[...] = fin_land[...]

    @pl.when(jnp.logical_not(away))
    def _():
        grad_out[...] = fin[...]

    for d in range(NDP - 1):
        drain(tok.at[0, my_rows, :], a1_send.at[d])
    for p in dests:
        drain(tok.at[0, pl.ds(0, 3 * share), :], a2_send.at[p])
        drain(tok.at[0, pl.ds(0, rows // 2), :], a3_send.at[p])
    drain(pin_send.at[pl.ds(0, NT - 1)], ps_send)
    drain(pin_all.at[pl.ds(0, NT - 1)], pa_send)
    drain(feat_send.at[pl.ds(0, NT - 1)], ft_send)

    def left(r, c):
        sl = at_round(r)
        for k in range(3):
            drain(part.at[k, :, sl, :], red_send.at[k, r])

            @pl.when(mid)
            def _():
                drain(part.at[k, :, sl, :], fwd_send.at[k, r])

        @pl.when(z < NDP - 1)
        def _():
            drain(part.at[0, :, sl, :], root_send.at[0, r])

        @pl.when(z > 0)
        def _():
            drain(part.at[0, :, sl, :], root_send.at[1, r])

        return c

    lax.fori_loop(0, rounds, left, 0)

    def left_rs(b, c):
        drain(term.at[pl.ds(0, NT - 1), at_block(b), :], rs_send.at[b])
        return c

    lax.fori_loop(0, blocks, left_rs, 0)


def fused_call(tokens, hidden_grad, gate_weight, up_weight, proj_in, proj_out):
    rows, width = tokens.shape
    block, hid = gate_weight.shape
    rank = proj_in.shape[2]
    band = width // NT
    rounds = rows // ROUND
    dma = pltpu.SemaphoreType.DMA
    vmem = pl.BlockSpec(memory_space=pltpu.VMEM)
    hbm = pl.BlockSpec(memory_space=pl.ANY)
    small = pltpu.VMEM((NT, 2, rank // NT, 128), F32)
    wide = (2, rows, hid)
    return pl.pallas_call(
        fused,
        out_shape=(
            jax.ShapeDtypeStruct((rows, band), BF16),
            jax.ShapeDtypeStruct((1, 2, rank // NT, rank), F32),
        ),
        in_specs=[vmem, vmem, hbm, hbm, vmem, vmem],
        out_specs=(vmem, vmem),
        scratch_shapes=[
            pltpu.VMEM((block, hid), BF16),
            pltpu.VMEM((block, hid), BF16),
            pltpu.VMEM((NDP, rows, block), BF16),
            pltpu.VMEM((NDP,) + wide, F32),
            pltpu.VMEM((3,) + wide, BF16),
            pltpu.VMEM((5,) + wide, BF16),
            pltpu.VMEM((NDP,) + wide, BF16),
            pltpu.VMEM((NT, rows, band), BF16),
            pltpu.VMEM((NT, rows, band), BF16),
            pltpu.VMEM((rows, band), BF16),
            pltpu.VMEM((rows, band), BF16),
            small, small, small, small, small,
            dma((2,)), dma((3,)), dma((NDP,)), dma((NDP,)), dma((NDP,)), dma((NDP,)), dma((NDP,)),
            dma((3, rounds)), dma((5, rounds)), dma((2, rounds)), dma((3, rounds)),
            dma((NDP, rounds)), dma((rounds // 2,)), dma((rounds // 2,)),
            dma((rounds // 2,)), dma((rounds // 2,)),
            dma(()), dma(()), dma(()), dma(()), dma(()), dma(()),
        ],
        compiler_params=pltpu.CompilerParams(
            collective_id=0, has_side_effects=True, vmem_limit_bytes=60 * 2**20
        ),
        cost_estimate=pl.CostEstimate(
            flops=16 * rows * NDP * block * hid // 2, bytes_accessed=8 * block * hid, transcendentals=rows * hid
        ),
    )(tokens, hidden_grad, gate_weight, up_weight, proj_in, proj_out)


def fits(mesh, tokens, gate_weight, proj_in):
    n_dp, n_tensor = mesh.shape["dp"], mesh.shape["tensor"]
    rows, width = tokens.shape[0] // n_dp, tokens.shape[1]
    hid = gate_weight.shape[1] // n_tensor
    return (
        (n_dp, n_tensor) == (NDP, NT)
        and rows == SEQ_LEN
        and width % (NT * TILE) == 0
        and hid % TILE == 0
        and proj_in.shape[2] == 64
    )


def solution(mesh):
    placed = (
        P("dp", None),
        P("dp", "tensor"),
        P("dp", "tensor"),
        P("dp", "tensor"),
        P(None, "tensor", None),
        P(None, "tensor", None),
    )

    def program(*args):
        if fits(mesh, args[0], args[2], args[4]):
            body = fused_call
        else:
            body = functools.partial(shards, mesh.shape["dp"], mesh.shape["tensor"])
        return jax.shard_map(
            body,
            mesh=mesh,
            in_specs=placed,
            out_specs=(P("dp", "tensor"), P("dp", None, "tensor", None)),
            check_vma=False,
        )(*args)

    return program
```
